32 devices in a mesh: dp: 8 (over z, y), seq: 4 (over x, core).
Axes of the slice: x: 2, y: 2, z: 4, core: 2. Of those that a mesh axis runs over, the one named last changes fastest.
Arguments:
- latents: bfloat16 [16384, 3072], P(('dp', 'seq')), may hold values from -6 to 6
- target: int32 [16384], P(('dp', 'seq')), may hold values from 0 to 16383, as said below
- segment_ids: int32 [8, 2048], P('dp', 'seq'), may hold values from 0 to 7, never falling along the last dimension, each value on 1 to 512 neighbouring positions
- clip_bucket: int32 [8, 8], P('dp'), may hold values from 0 to 15
- mod_table: bfloat16 [16, 6144], replicated, may hold values from -3 to 3
- w_query: bfloat16 [3072, 1536], P('dp', 'seq')
- w_key: bfloat16 [3072, 1536], P('dp', 'seq')
- w_value: bfloat16 [3072, 1536], P('dp', 'seq'), may hold values from -0.109375 to 0.109375
Outputs:
- attended: bfloat16 [16384, 1536], P(('dp', 'seq'))
The draws below stay inside these ranges and needn't reach their ends.
Inputs may be any that keep to these rules, and one draw needn't show every extreme that they name: `target`: a permutation of 0 to 16383; a token stays at the same index of seq; a device sends at most 96 tokens to one index of dp, exactly 96 to some index in every draw, and sends to at most (607) // 96 + 1 indices.
All inputs are finite; a program needn't handle non-finite values.
Results may differ from the reference program's by a relative error of at most 0.0051.
Values may be sent and summed in bfloat16 or wider, within the bound.
No kernel may reach another device: no remote copies, remote signals or barrier semaphores. Data moves between devices by JAX's collectives and lax.ppermute only.
A program may use at most 128 MiB of HBM per device.

```python
import math
import jax
import jax.numpy as jnp
import numpy as np
from jax import lax

D = 3072
HEADS = 12
HEAD_DIM = 128
CLIPS = 8
BUCKETS = 16
TOK_DEV = 512
SEQ_LEN = 2048
TOKENS = 16384
CAP = 96
N_DP = 8
N_SEQ = 4


def shared_rows(key):
    return jax.random.normal(key, (D, HEADS * HEAD_DIM), jnp.float32) * D ** (-0.5)


def draw_w_query(key, part):
    shared = shared_rows(key)
    return shared.astype(jnp.bfloat16)


def draw_w_key(key, part):
    key = jax.random.fold_in(key, 7)
    independent = jax.random.normal(key, (D, HEADS * HEAD_DIM), jnp.float32) * D ** (-0.5)
    return independent.astype(jnp.bfloat16)


def plan_column(key, column):
    subkeys = jax.random.split(key, 3)
    route_count = (TOK_DEV + CAP - 1) // CAP + 1
    shifts = jax.random.permutation(subkeys[0], N_DP)[:route_count]
    remaining = TOK_DEV - CAP
    base_count = remaining // (route_count - 1)
    extra_count = remaining % (route_count - 1)
    later = base_count + (jnp.arange(route_count - 1) < extra_count).astype(jnp.int32)
    counts = jnp.concatenate([jnp.full((1,), CAP, jnp.int32), later.astype(jnp.int32)])
    group_ends = jnp.cumsum(counts)
    ordered = jnp.arange(TOK_DEV)
    group_of = jnp.sum((ordered[:, None] >= group_ends[None, :]).astype(jnp.int32), axis=1)
    senders = jnp.arange(N_DP)
    receiver = (senders[:, None] + shifts[group_of][None, :]) % N_DP
    source_rows = jax.vmap(lambda sub: jax.random.permutation(sub, TOK_DEV))(jax.random.split(subkeys[1], N_DP))
    final_rows = jax.vmap(lambda sub: jax.random.permutation(sub, TOK_DEV))(jax.random.split(subkeys[2], N_DP))
    landing = final_rows[receiver, ordered[None, :]]
    landing_row = (receiver * N_SEQ + column) * TOK_DEV + landing
    plan_table = jnp.zeros((N_DP, TOK_DEV), jnp.int32)
    plan_table = plan_table.at[senders[:, None], source_rows].set(landing_row.astype(jnp.int32))
    return plan_table


def draw_target(key, part):
    key = jax.random.fold_in(key, 3)
    columns = [plan_column(jax.random.fold_in(key, column), column) for column in range(N_SEQ)]
    stacked = jnp.stack(columns, axis=1)
    return stacked.reshape(N_DP * N_SEQ * TOK_DEV)


def with_ends(values, own_key, least, largest):
    longest = values.shape.index(max(values.shape))
    spots = []
    for shift in (0, 1):
        where = [jax.random.randint(jax.random.fold_in(own_key, axis), (), 0, length) for axis, length in enumerate(values.shape)]
        where[longest] = (where[longest] + shift) % values.shape[longest]
        spots.append(tuple(where))
    return values.at[spots[0]].set(least).at[spots[1]].set(largest)


def block_levels(key, extent, cuts, low, largest):
    def one(dim, blocks):
        steps = jax.random.uniform(jax.random.fold_in(jax.random.fold_in(key, 6), dim), (blocks,), jnp.float32, low / len(cuts), largest / len(cuts))
        return jnp.repeat(jnp.exp(steps), extent[dim] // blocks).reshape((-1,) + (1,) * (len(extent) - dim - 1))

    loudness = one(*cuts[0])
    for cut in cuts[1:]:
        loudness = loudness * one(*cut)
    return loudness


def split_up(amount, total, bound, lean):
    portions = [(1 << 20) // math.isqrt(standing ** lean) + 1 for standing in range(2, amount + 1)]
    spare, given = total - bound - (amount - 1), [1] * (amount - 1)
    while spare > 0:
        candidates = [i for i in range(amount - 1) if given[i] < bound]
        pool, left = sum([portions[i] for i in candidates]), spare
        for i in candidates:
            more = min(bound - given[i], max(1, left * portions[i] // pool), spare)
            given[i] = given[i] + more
            spare = spare - more
    return np.array([bound] + given)


def uneven_parts(key, count, total, most, slope):
    if count == 2:
        one = jax.random.randint(key, (), max(1, total - most), min(most, total - 1) + 1)
        return jnp.stack([one, total - one])
    tallies = jnp.asarray(split_up(count, total, most, slope), jnp.int32)
    pairs = (count - 1) // 2
    giver, taker = tallies[1:1 + 2 * pairs:2], tallies[2:2 + 2 * pairs:2]
    room = jnp.minimum(giver - 1, most - taker)
    shifted = jax.random.randint(jax.random.fold_in(key, 1), (pairs,), 0, 1 << 20) % (room + 1)
    tallies = tallies.at[1:1 + 2 * pairs:2].set(giver - shifted).at[2:2 + 2 * pairs:2].set(taker + shifted)
    return tallies[jax.random.permutation(jax.random.fold_in(key, 2), count)]


def normal_values(stream_key, shape, spread, limit, cuts=(), held_as=jnp.bfloat16):
    entries = spread * jax.random.normal(stream_key, shape, jnp.float32)
    if cuts:
        entries = entries * block_levels(stream_key, shape, cuts, -0.22, 0.18)
    return jnp.clip(entries, -limit, limit).astype(held_as)


def setup_inputs(seed: int = 0) -> dict:
    seeds = jax.random.split(jax.random.key(seed), 9)
    return {
        "latents": normal_values(seeds[0], (TOKENS, D), 1.0, 6.0, ((0, 32),)),
        "target": draw_target(jax.random.fold_in(seeds[8], 71), 0),
        "segment_ids": jax.vmap(lambda own: jnp.searchsorted(jnp.cumsum(uneven_parts(own, CLIPS, SEQ_LEN, SEQ_LEN // 4, 2)), jnp.arange(SEQ_LEN), side="right"))(jax.random.split(seeds[2], N_DP)).reshape((N_DP, SEQ_LEN)).astype(jnp.int32),
        "clip_bucket": with_ends(jax.random.randint(seeds[3], (N_DP, CLIPS), 0, BUCKETS), jax.random.fold_in(seeds[3], 1), 0, BUCKETS - 1).astype(jnp.int32),
        "mod_table": normal_values(seeds[4], (BUCKETS, 2 * D), 0.5, 3.0),
        "w_query": draw_w_query(jax.random.fold_in(seeds[8], 71), 0),
        "w_key": draw_w_key(jax.random.fold_in(seeds[8], 71), 0),
        "w_value": normal_values(seeds[7], (D, HEADS * HEAD_DIM), D ** -0.5, 0.109375, ((0, 8), (1, 4))),
    }


def modulated_norm(latent_rows, token_bucket, mod_table):
    width = latent_rows.shape[1]
    modulation = mod_table[token_bucket].astype(jnp.float32)
    shift_part = modulation[:, :width]
    scale_part = modulation[:, width:]
    widened = latent_rows.astype(jnp.float32)
    row_mean = lax.optimization_barrier(jnp.mean(widened, axis=1, keepdims=True))
    centered = widened - row_mean
    row_var = lax.optimization_barrier(jnp.mean(centered * centered, axis=1, keepdims=True))
    normalized = centered * lax.rsqrt(row_var + 1e-06)
    return (normalized * (1.0 + scale_part) + shift_part).astype(jnp.bfloat16)

def reference(latents, target, segment_ids, clip_bucket, mod_table, w_query, w_key, w_value):
    placed = jnp.zeros_like(latents).at[target].set(latents)
    grouped = placed.reshape(N_DP, SEQ_LEN, D)
    factor = HEAD_DIM ** (-0.5)

    def group_attention(inputs):
        latent_rows, segment_row, bucket_row = inputs
        token_bucket = bucket_row[segment_row]
        hidden = modulated_norm(latent_rows, token_bucket, mod_table)
        query = jnp.dot(hidden, w_query, preferred_element_type=jnp.float32).astype(jnp.bfloat16)
        keys = jnp.dot(hidden, w_key, preferred_element_type=jnp.float32).astype(jnp.bfloat16)
        values = jnp.dot(hidden, w_value, preferred_element_type=jnp.float32).astype(jnp.bfloat16)
        query = query.reshape(SEQ_LEN, HEADS, HEAD_DIM).astype(jnp.float32)
        keys = keys.reshape(SEQ_LEN, HEADS, HEAD_DIM).astype(jnp.float32)
        values = values.reshape(SEQ_LEN, HEADS, HEAD_DIM).astype(jnp.float32)
        scores = jnp.einsum('qhd,khd->hqk', query, keys) * factor
        same_clip = segment_row[:, None] == segment_row[None, :]
        scores = jnp.where(same_clip[None, :, :], scores, -1e+30)
        row_max = lax.optimization_barrier(jnp.max(scores, axis=2, keepdims=True))
        exponent = jnp.exp(scores - row_max)
        row_total = lax.optimization_barrier(jnp.sum(exponent, axis=2, keepdims=True))
        probs = (exponent / row_total).astype(jnp.bfloat16)
        result = jnp.einsum('hqk,khd->qhd', probs.astype(jnp.float32), values)
        return result.reshape(SEQ_LEN, HEADS * HEAD_DIM).astype(jnp.bfloat16)
    attended = lax.map(group_attention, (grouped, segment_ids, clip_bucket))
    return attended.reshape(TOKENS, HEADS * HEAD_DIM)
```

```python
import functools

import jax
import jax.numpy as jnp
from jax import lax
from jax.experimental import pallas as pl
from jax.experimental.pallas import tpu as pltpu
from jax.sharding import PartitionSpec as P

HEAD_DIM = 128
TILE = 256
LANES = 128
MOST = 512
BLOCKED = -(2.0**100)


def params(mebibytes):
    return pltpu.CompilerParams(vmem_limit_bytes=mebibytes * 1024 * 1024)


def cost(flops, moved):
    return pl.CostEstimate(flops=int(flops), bytes_accessed=int(moved), transcendentals=0)


def one_hot(found):
    return found.astype(jnp.float32).astype(jnp.bfloat16)


def pack_kernel(me_ref, target_ref, latents_ref, *out_refs, seq_count):
    group_count = len(out_refs)
    capacity = out_refs[0].shape[0]
    local_rows, width = latents_ref.shape
    target = target_ref[...]
    dest = target // (seq_count * local_rows)
    row = target % local_rows
    groups = lax.broadcasted_iota(jnp.int32, (max(16, group_count), local_rows), 0)
    hit = (groups == dest).astype(jnp.float32)
    before = lax.broadcasted_iota(jnp.int32, (local_rows, local_rows), 0)
    after = lax.broadcasted_iota(jnp.int32, (local_rows, local_rows), 1)
    ranks = jnp.dot(
        hit.astype(jnp.bfloat16), one_hot(before < after), preferred_element_type=jnp.float32
    )
    rank = jnp.sum(hit * ranks, axis=0, keepdims=True).astype(jnp.int32)
    slots = lax.bitwise_xor(dest, me_ref[0]) * capacity + rank
    wanted = lax.broadcasted_iota(jnp.int32, (group_count * capacity, local_rows), 0)
    pick = one_hot(wanted == slots)
    lines = lax.broadcasted_iota(jnp.int32, (LANES, local_rows), 0)
    places = jnp.where(lines == 0, row // 16, jnp.where(lines == 1, row % 16, 1))
    places = places.astype(jnp.float32).astype(jnp.bfloat16)

    def store(columns, result):
        result = result.astype(jnp.bfloat16)
        for relative, out_ref in enumerate(out_refs):
            out_ref[:, columns] = result[relative * capacity : (relative + 1) * capacity]

    store(
        slice(width, width + LANES),
        lax.dot_general(pick, places, (((1,), (1,)), ((), ())), preferred_element_type=jnp.float32),
    )
    step = 512
    for start in range(0, width, step):
        columns = slice(start, start + step)
        store(
            columns, jnp.dot(pick, latents_ref[:, columns], preferred_element_type=jnp.float32)
        )


def pack(me, target, latents, group_count, seq_count, capacity):
    width = latents.shape[1] + LANES
    whole = pl.BlockSpec(memory_space=pltpu.VMEM)
    return pl.pallas_call(
        functools.partial(pack_kernel, seq_count=seq_count),
        in_specs=[pl.BlockSpec(memory_space=pltpu.SMEM), whole, whole],
        out_specs=[whole] * group_count,
        out_shape=[jax.ShapeDtypeStruct((capacity, width), jnp.bfloat16)] * group_count,
        compiler_params=params(24),
        cost_estimate=cost(
            2 * group_count * capacity * latents.size, 2 * width * (group_count * capacity + latents.shape[0])
        ),
        name="pack",
    )(me, target[None, :], latents)


def join_kernel(*refs):
    out_ref = refs[-1]
    start = 0
    for ref in refs[:-1]:
        out_ref[:, start : start + ref.shape[1]] = ref[...]
        start += ref.shape[1]


def join(arrays):
    rows = arrays[0].shape[0]
    columns = sum(array.shape[1] for array in arrays)
    whole = pl.BlockSpec(memory_space=pltpu.VMEM)
    return pl.pallas_call(
        join_kernel,
        in_specs=[whole] * len(arrays),
        out_specs=whole,
        out_shape=jax.ShapeDtypeStruct((rows, columns), arrays[0].dtype),
        compiler_params=params(8),
        cost_estimate=cost(0, 0),
        name="join",
    )(*arrays)


def marks_kernel(me_ref, *refs, per_block):
    segment_refs, (meta_ref, other_ref, clip_ref) = refs[:-3], refs[-3:]
    tiles = len(segment_refs) * per_block
    every = jnp.concatenate([ref[...] for ref in segment_refs], axis=0)
    lines = lax.broadcasted_iota(jnp.int32, (16, TILE), 0)
    lanes = lax.broadcasted_iota(jnp.int32, (16, LANES), 1)
    unit = one_hot(lax.broadcasted_iota(jnp.int32, (16, LANES), 0) == lanes)
    for tile in range(tiles):
        relative, chunk = tile // per_block, tile % per_block
        mine = segment_refs[relative][:, chunk * TILE : (chunk + 1) * TILE]
        meta_ref[tile] = jnp.sum((every < jnp.min(mine)).astype(jnp.int32))
        meta_ref[tiles + tile] = jnp.sum((every <= jnp.max(mine)).astype(jnp.int32))
        hit = lax.dot_general(
            one_hot(lines == mine), unit, (((0,), (0,)), ((), ())), preferred_element_type=jnp.float32
        )
        used = lax.broadcasted_iota(jnp.int32, (TILE, LANES), 1) < 16
        other_ref[tile] = jnp.where(used & (hit < 0.5), BLOCKED, 0.0).astype(jnp.bfloat16)
        place = lax.bitwise_xor(me_ref[0], relative) * per_block + chunk
        clip_ref[pl.ds(pl.multiple_of(place * TILE, TILE), TILE), :] = hit.astype(jnp.bfloat16)


def marks(me, segments, per_block):
    whole = pl.BlockSpec(memory_space=pltpu.VMEM)
    scalars = pl.BlockSpec(memory_space=pltpu.SMEM)
    tiles = len(segments) * per_block
    return pl.pallas_call(
        functools.partial(marks_kernel, per_block=per_block),
        in_specs=[scalars] + [whole] * len(segments),
        out_specs=[scalars, whole, whole],
        out_shape=[
            jax.ShapeDtypeStruct((2 * tiles,), jnp.int32),
            jax.ShapeDtypeStruct((tiles, TILE, LANES), jnp.bfloat16),
            jax.ShapeDtypeStruct((tiles * TILE, LANES), jnp.bfloat16),
        ],
        compiler_params=params(8),
        cost_estimate=cost(0, 0),
        name="marks",
    )(me, *segments)


def place_kernel(clip_bucket_ref, segment_ref, table_ref, *refs, start):
    incoming_refs, refs = refs[:-5], refs[-5:]
    out_ref, *half_refs, held_ref, sems = refs
    tile, width = out_ref.shape
    slots = held_ref.shape[0]
    capacity = incoming_refs[0].shape[0]
    buckets = table_ref.shape[0]

    @pl.when(pl.program_id(0) == 0)
    def _():
        copies = [
            pltpu.make_async_copy(ref, held_ref.at[pl.ds(i * capacity, capacity)], sems.at[i])
            for i, ref in enumerate(incoming_refs)
        ]
        for copy in copies:
            copy.start()
        for copy in copies:
            copy.wait()

    lines = lax.broadcasted_iota(jnp.int32, (16, LANES), 0)
    lanes = lax.broadcasted_iota(jnp.int32, (16, LANES), 1)
    reader = jnp.where(lines == 0, jnp.where(lanes == 0, 16, jnp.where(lanes == 1, 1, 0)), 0)
    reader = jnp.where((lines == 1) & (lanes == 2), 1, reader)
    found = lax.dot_general(
        reader.astype(jnp.float32).astype(jnp.bfloat16),
        held_ref[:, width:],
        (((1,), (1,)), ((), ())),
        preferred_element_type=jnp.float32,
    ).astype(jnp.int32)
    rows = jnp.where(found[1:2] > 0, found[0:1], -1)
    first = pl.program_id(0) * tile + start
    mine = lax.broadcasted_iota(jnp.int32, (tile, slots), 0) + first
    pick = one_hot(mine == rows)
    placed = jnp.dot(pick, held_ref[:, :width], preferred_element_type=jnp.float32)
    row_mean = jnp.mean(placed, axis=1, keepdims=True)
    centered = placed - row_mean
    row_var = jnp.mean(centered * centered, axis=1, keepdims=True)
    normalized = centered * lax.rsqrt(row_var + 1e-06)
    lines = lax.broadcasted_iota(jnp.int32, (16, buckets), 0)
    bucket_of = jnp.full((16, buckets), -1, jnp.int32)
    for clip in range(clip_bucket_ref.shape[1]):
        bucket_of = jnp.where(lines == clip, clip_bucket_ref[0, clip], bucket_of)
    clip_hit = lax.broadcasted_iota(jnp.int32, (16, tile), 0) == segment_ref[...]
    bucket_hit = lax.dot_general(
        one_hot(clip_hit),
        one_hot(bucket_of == lax.broadcasted_iota(jnp.int32, (16, buckets), 1)),
        (((0,), (0,)), ((), ())),
        preferred_element_type=jnp.float32,
    ).astype(jnp.bfloat16)
    shift = jnp.dot(bucket_hit, table_ref[:, :width], preferred_element_type=jnp.float32)
    scale = jnp.dot(bucket_hit, table_ref[:, width:], preferred_element_type=jnp.float32)
    result = (normalized * (1.0 + scale) + shift).astype(jnp.bfloat16)
    out_ref[...] = result
    for which, half_ref in enumerate(half_refs):

        @pl.when(pl.program_id(0) == which)
        def _():
            half_ref[...] = result


def place_and_norm(clip_bucket, segments, incoming, mod_table, start, tile):
    capacity, wide = incoming[0].shape
    width = wide - LANES
    slots = capacity * len(incoming)
    first = start // tile
    return pl.pallas_call(
        functools.partial(place_kernel, start=start),
        grid=(2,),
        in_specs=[
            pl.BlockSpec(memory_space=pltpu.SMEM),
            pl.BlockSpec((1, tile), lambda i: (0, i + first)),
            pl.BlockSpec(mod_table.shape, lambda i: (0, 0)),
        ]
        + [pl.BlockSpec(memory_space=pl.ANY)] * len(incoming),
        out_specs=[pl.BlockSpec((tile, width), lambda i: (i, 0))]
        + [pl.BlockSpec((tile, width), lambda i: (0, 0))] * 2,
        out_shape=[jax.ShapeDtypeStruct((2 * tile, width), jnp.bfloat16)]
        + [jax.ShapeDtypeStruct((tile, width), jnp.bfloat16)] * 2,
        scratch_shapes=[
            pltpu.VMEM((slots, wide), jnp.bfloat16),
            pltpu.SemaphoreType.DMA((len(incoming),)),
        ],
        compiler_params=params(20),
        cost_estimate=cost(0, 0),
        name="place_and_norm",
    )(clip_bucket, segments, mod_table, *incoming)


def attend_tile(first, last, query, other, key_ref, value_ref, clip_ref, write):
    length = key_ref.shape[0]
    tile, columns = query.shape
    heads = columns // HEAD_DIM
    factor = (HEAD_DIM ** (-0.5)) * 1.4426950408889634
    reach = min(length, (tile - 1 + 2 * (MOST - 1) + 2 * LANES - 1) // LANES * LANES)
    sizes = [size for size in (512, 768, 1024) if size < reach] + [reach]
    first = first // LANES * LANES
    need = last - first

    def work(size):
        start = pl.multiple_of(jnp.clip(first, 0, length - size), LANES)
        clip = clip_ref[pl.ds(start, size), :]

        def score(head):
            lanes = slice(head * HEAD_DIM, (head + 1) * HEAD_DIM)
            return lax.dot_general(
                jnp.concatenate([key_ref[pl.ds(start, size), lanes], clip], axis=1),
                jnp.concatenate([query[:, lanes], other], axis=1),
                (((1,), (1,)), ((), ())),
                preferred_element_type=jnp.float32,
            )

        def finish(head, scores):
            lanes = slice(head * HEAD_DIM, (head + 1) * HEAD_DIM)
            top = jnp.max(scores, axis=0, keepdims=True)
            weights = jnp.exp2((scores - top) * factor)
            total = jnp.sum(weights, axis=0, keepdims=True)
            mixed = jnp.dot(
                value_ref[lanes, pl.ds(start, size)],
                weights.astype(jnp.bfloat16),
                preferred_element_type=jnp.float32,
            )
            write(lanes, (mixed / total).T.astype(jnp.bfloat16))

        scores = score(0)
        for head in range(heads):
            following = score(head + 1) if head + 1 < heads else None
            finish(head, scores)
            scores = following

    least = 0
    for size in sizes:

        @pl.when((need > least) & (need <= size))
        def _():
            work(size)

        least = size


def load_parts(part_refs, part_rows, hidden, sems, block):
    copies, start = [], 0
    for count, ref in zip(part_rows, part_refs):
        spot = hidden.at[pl.ds(start, count)]
        copies.append(pltpu.make_async_copy(ref, spot, sems.at[start // block]))
        start += count
    return copies


def arrived(hidden, sems, group, block):
    spot = pl.ds(pl.multiple_of(group * block, block), block)
    pltpu.make_async_copy(hidden.at[spot], hidden.at[spot], sems.at[group]).wait()
    return hidden.at[spot]


def halves(me_ref, half, depth):
    near_start = pl.multiple_of(me_ref[0] // half * depth, depth)
    return near_start, pl.multiple_of(depth - near_start, depth)


def near_half_kernel(me_ref, *refs, part_count):
    part_refs, refs = refs[:part_count], refs[part_count:]
    piece_refs, (weights, total, hidden, hidden_sems, weight_sems) = refs[:-5], refs[-5:]
    rows = piece_refs[0].shape[0]
    half = len(piece_refs)
    near_start, _ = halves(me_ref, half, half * rows)
    copies = []
    for relative, ref in enumerate(piece_refs):
        place = lax.bitwise_xor(me_ref[0], relative) % half * rows
        spot = weights.at[pl.ds(pl.multiple_of(place, rows), rows)]
        copies.append(pltpu.make_async_copy(ref, spot, weight_sems.at[relative]))
    count = part_refs[0].shape[0]
    for i, ref in enumerate(part_refs):
        spot = hidden.at[pl.ds(i * count, count)]
        source = ref.at[:, pl.ds(near_start, half * rows)]
        copies.append(pltpu.make_async_copy(source, spot, hidden_sems.at[i]))
    for copy in copies:
        copy.start()
    for copy in copies:
        copy.wait()
    total[...] = jnp.dot(hidden[...], weights[...], preferred_element_type=jnp.float32)


def near_half(me, parts, pieces):
    rows, all_columns = pieces[0].shape
    depth = rows * len(pieces)
    block = sum(part.shape[0] for part in parts)
    anywhere = pl.BlockSpec(memory_space=pl.ANY)
    whole = pl.BlockSpec(memory_space=pltpu.VMEM)
    return pl.pallas_call(
        functools.partial(near_half_kernel, part_count=len(parts)),
        in_specs=[pl.BlockSpec(memory_space=pltpu.SMEM)] + [anywhere] * (len(parts) + len(pieces)),
        out_specs=[whole] * 2,
        out_shape=[
            jax.ShapeDtypeStruct((depth, all_columns), jnp.bfloat16),
            jax.ShapeDtypeStruct((block, all_columns), jnp.float32),
        ],
        scratch_shapes=[
            pltpu.VMEM((block, depth), jnp.bfloat16),
            pltpu.SemaphoreType.DMA((len(parts),)),
            pltpu.SemaphoreType.DMA((len(pieces),)),
        ],
        compiler_params=params(16),
        cost_estimate=cost(2 * block * depth * all_columns, 0),
        name="near_half",
    )(me, *parts, *pieces)


def first_kernel(me_ref, near_weights, begun, *refs, own_count, part_rows, per_block):
    own_refs, refs = refs[:own_count], refs[own_count:]
    part_refs, refs = refs[: len(part_rows)], refs[len(part_rows) :]
    piece_refs, refs = refs[:-8], refs[-8:]
    weights, queries, keys, values, own, hidden, part_sems, weight_sems = refs
    rows = piece_refs[0].shape[0]
    columns = keys.shape[2]
    half = len(piece_refs)
    depth = half * rows
    near_start, far_start = halves(me_ref, half, depth)
    pieces = []
    for i, ref in enumerate(piece_refs):
        place = lax.bitwise_xor(me_ref[0], half + i) % half * rows
        spot = weights.at[pl.ds(pl.multiple_of(place, rows), rows)]
        pieces.append(pltpu.make_async_copy(ref, spot, weight_sems.at[i]))
    block = per_block * TILE
    parts = load_parts(part_refs, part_rows, hidden, part_sems, block)
    count = own_refs[0].shape[0]
    owns = []
    for i, ref in enumerate(own_refs):
        spot = own.at[pl.ds(i * count, count)]
        source = ref.at[:, pl.ds(far_start, depth)]
        owns.append(pltpu.make_async_copy(source, spot, part_sems.at[1 + i]))
    for copy in parts + pieces + owns:
        copy.start()

    def store(group, whole):
        keys[group] = whole[:, columns : 2 * columns].astype(jnp.bfloat16)
        values[group] = whole[:, 2 * columns :].T.astype(jnp.bfloat16)
        for i in range(per_block):
            queries[group * per_block + i] = whole[i * TILE : (i + 1) * TILE, :columns].astype(
                jnp.bfloat16
            )

    mine = arrived(hidden, part_sems, 0, block)
    total = jnp.dot(
        mine[:, pl.ds(near_start, depth)], near_weights[...], preferred_element_type=jnp.float32
    )
    for copy in pieces:
        copy.wait()
    total += jnp.dot(
        mine[:, pl.ds(far_start, depth)], weights[...], preferred_element_type=jnp.float32
    )
    store(1, total)
    for copy in owns:
        copy.wait()
    store(0, begun[...] + jnp.dot(own[...], weights[...], preferred_element_type=jnp.float32))


def project_first(me, near_weights, begun, own_parts, parts, pieces, per_block):
    width = parts[0].shape[1]
    rows, all_columns = pieces[0].shape
    depth = rows * len(pieces)
    columns = all_columns // 3
    block = per_block * TILE
    anywhere = pl.BlockSpec(memory_space=pl.ANY)
    whole = pl.BlockSpec(memory_space=pltpu.VMEM)
    return pl.pallas_call(
        functools.partial(
            first_kernel,
            own_count=len(own_parts),
            part_rows=[part.shape[0] for part in parts],
            per_block=per_block,
        ),
        in_specs=[pl.BlockSpec(memory_space=pltpu.SMEM), whole, whole]
        + [anywhere] * (len(own_parts) + len(parts) + len(pieces)),
        out_specs=[whole] * 4,
        out_shape=[
            jax.ShapeDtypeStruct((depth, all_columns), jnp.bfloat16),
            jax.ShapeDtypeStruct((2 * per_block, TILE, columns), jnp.bfloat16),
            jax.ShapeDtypeStruct((2, block, columns), jnp.bfloat16),
            jax.ShapeDtypeStruct((2, columns, block), jnp.bfloat16),
        ],
        scratch_shapes=[
            pltpu.VMEM((block, depth), jnp.bfloat16),
            pltpu.VMEM((block, width), jnp.bfloat16),
            pltpu.SemaphoreType.DMA((1 + len(own_parts),)),
            pltpu.SemaphoreType.DMA((len(pieces),)),
        ],
        compiler_params=params(22),
        cost_estimate=cost(4 * block * width * all_columns, 0),
        name="project_first",
    )(me, near_weights, begun, *own_parts, *parts, *pieces)


def project_kernel(
    me_ref,
    meta_ref,
    other_ref,
    clip_ref,
    near_weights,
    far_weights,
    first_queries,
    first_keys,
    first_values,
    *refs,
    part_rows,
    group_count,
    seq_count,
    per_block,
):
    side = seq_count // 2
    far_tiles = side * per_block
    part_refs, refs = refs[: len(part_rows)], refs[len(part_rows) :]
    far_refs, refs = refs[:side], refs[side:]
    queries, keys, values, hidden, far, hidden_sems, copy_sems = refs
    me_seq = me_ref[1]
    columns = keys.shape[1]
    depth = near_weights.shape[0]
    near_start, far_start = halves(me_ref, group_count // 2, depth)
    block = per_block * TILE
    tiles = seq_count * per_block
    parts = load_parts(part_refs, part_rows, hidden, hidden_sems, block)
    moves = []
    for group in range(side):
        place = pl.multiple_of(lax.bitwise_xor(me_seq, 2 * group) * block, block)
        moves += [
            (first_keys.at[group], keys.at[pl.ds(place, block)]),
            (first_values.at[group], values.at[:, pl.ds(place, block)]),
            (
                first_queries.at[pl.ds(group * per_block, per_block)],
                queries.at[pl.ds(2 * group * per_block, per_block)],
            ),
        ]
    moves = [
        pltpu.make_async_copy(source, place, copy_sems.at[i])
        for i, (source, place) in enumerate(moves)
    ]
    for copy in parts + moves:
        copy.start()

    def step(group, _):
        mine = arrived(hidden, hidden_sems, group, block)
        whole = jnp.dot(
            mine[:, pl.ds(near_start, depth)], near_weights[...], preferred_element_type=jnp.float32
        ) + jnp.dot(
            mine[:, pl.ds(far_start, depth)], far_weights[...], preferred_element_type=jnp.float32
        )
        relative = 2 * group + 1
        place = pl.multiple_of(lax.bitwise_xor(me_seq, relative) * block, block)
        keys[pl.ds(place, block), :] = whole[:, columns : 2 * columns].astype(jnp.bfloat16)
        values[:, pl.ds(place, block)] = whole[:, 2 * columns :].T.astype(jnp.bfloat16)
        for i in range(per_block):
            queries[relative * per_block + i] = whole[i * TILE : (i + 1) * TILE, :columns].astype(
                jnp.bfloat16
            )
        return 0

    lax.fori_loop(0, side, step, 0)
    for copy in moves:
        copy.wait()

    def far_step(i, _):
        tile = tiles - far_tiles + i

        def write(lanes, result):
            far[i, :, lanes] = result

        attend_tile(
            meta_ref[tile],
            meta_ref[tiles + tile],
            queries.at[tile],
            other_ref[tile],
            keys,
            values,
            clip_ref,
            write,
        )
        return 0

    lax.fori_loop(0, far_tiles, far_step, 0)
    for i, far_ref in enumerate(far_refs):
        for j in range(per_block):
            far_ref[j * TILE : (j + 1) * TILE, :] = far[i * per_block + j]


def project_and_attend(me, meta, other, clip, parts, first, group_count, seq_count, per_block):
    depth, all_columns = first[0].shape
    width = 2 * depth
    columns = all_columns // 3
    side = seq_count // 2
    tiles = seq_count * per_block
    length = tiles * TILE
    whole = pl.BlockSpec(memory_space=pltpu.VMEM)
    scalars = pl.BlockSpec(memory_space=pltpu.SMEM)
    return pl.pallas_call(
        functools.partial(
            project_kernel,
            part_rows=[part.shape[0] for part in parts],
            group_count=group_count,
            seq_count=seq_count,
            per_block=per_block,
        ),
        in_specs=[scalars, scalars]
        + [whole] * (2 + len(first))
        + [pl.BlockSpec(memory_space=pl.ANY)] * len(parts),
        out_specs=[whole] * (side + 3),
        out_shape=[jax.ShapeDtypeStruct((per_block * TILE, columns), jnp.bfloat16)] * side
        + [
            jax.ShapeDtypeStruct((tiles, TILE, columns), jnp.bfloat16),
            jax.ShapeDtypeStruct((length, columns), jnp.bfloat16),
            jax.ShapeDtypeStruct((columns, length), jnp.bfloat16),
        ],
        scratch_shapes=[
            pltpu.VMEM((length // 2, width), jnp.bfloat16),
            pltpu.VMEM((side * per_block, TILE, columns), jnp.bfloat16),
            pltpu.SemaphoreType.DMA((side,)),
            pltpu.SemaphoreType.DMA((3 * side,)),
        ],
        compiler_params=params(22),
        cost_estimate=cost(2 * length * width * all_columns, 0),
        name="project_and_attend",
    )(me, meta, other, clip, *first, *parts)


def near_kernel(meta_ref, other_ref, query_ref, key_ref, value_ref, clip_ref, *refs):
    out_refs, result_ref = refs[:-1], refs[-1]
    index = pl.program_id(0)
    tiles = meta_ref.shape[0] // 2

    def write(lanes, result):
        result_ref[:, lanes] = result

    attend_tile(
        meta_ref[index],
        meta_ref[tiles + index],
        query_ref.at[0],
        other_ref[0],
        key_ref,
        value_ref,
        clip_ref,
        write,
    )
    for which, out_ref in enumerate(out_refs):

        @pl.when(index == which)
        def _():
            out_ref[...] = result_ref[...]


def attend_near(meta, other, query, keys, values, clip, tiles):
    _, tile, columns = query.shape

    def whole(array):
        return pl.BlockSpec(array.shape, lambda i, meta: (0, 0))

    return pl.pallas_call(
        near_kernel,
        grid_spec=pltpu.PrefetchScalarGridSpec(
            num_scalar_prefetch=1,
            grid=(tiles,),
            in_specs=[
                pl.BlockSpec((1, tile, LANES), lambda i, meta: (i, 0, 0)),
                pl.BlockSpec((1, tile, columns), lambda i, meta: (i, 0, 0)),
                whole(keys),
                whole(values),
                whole(clip),
            ],
            out_specs=[pl.BlockSpec((tile, columns), lambda i, meta: (0, 0))] * tiles,
            scratch_shapes=[pltpu.VMEM((tile, columns), jnp.bfloat16)],
        ),
        out_shape=[jax.ShapeDtypeStruct((tile, columns), jnp.bfloat16)] * tiles,
        compiler_params=params(20),
        cost_estimate=cost(8 * query.size * keys.shape[0], 6 * keys.size),
        name="attend_near",
    )(meta, other, query, keys, values, clip)


def order_kernel(me_ref, *refs, counts):
    part_refs, out_ref = refs[:-1], refs[-1]
    column = pl.program_id(0)
    for relative, count in enumerate(counts):
        mine, part_refs = part_refs[:count], part_refs[count:]

        @pl.when(lax.bitwise_xor(column, me_ref[0]) == relative)
        def _():
            start = 0
            for part in mine:
                out_ref[start : start + part.shape[0], :] = part[...]
                start += part.shape[0]


def side_by_side(me, parts):
    rows = sum(part.shape[0] for part in parts[0])
    columns = parts[0][0].shape[1]
    flat = [part for group in parts for part in group]
    return pl.pallas_call(
        functools.partial(order_kernel, counts=[len(group) for group in parts]),
        grid_spec=pltpu.PrefetchScalarGridSpec(
            num_scalar_prefetch=1,
            grid=(len(parts),),
            in_specs=[pl.BlockSpec(part.shape, lambda i, me: (0, 0)) for part in flat],
            out_specs=pl.BlockSpec((rows, columns), lambda i, me: (0, i)),
        ),
        out_shape=jax.ShapeDtypeStruct((rows, columns * len(parts)), jnp.bfloat16),
        compiler_params=params(12),
        cost_estimate=cost(0, 4 * rows * columns * len(parts)),
        name="side_by_side",
    )(me, *flat)


def swap(value, axis, distance):
    count = lax.axis_size(axis)
    return lax.ppermute(value, axis, [(i, i ^ distance) for i in range(count)])


def swap_gather(blocks, axis, distance):
    blocks = dict(blocks)
    while distance:
        for relative in sorted(blocks):
            blocks[relative ^ distance] = swap(blocks[relative], axis, distance)
        distance //= 2
    return blocks


def after(value, *others):
    return lax.optimization_barrier((value, *others))[0]


def on_device(latents, target, segment_ids, clip_bucket, mod_table, w_query, w_key, w_value):
    local_rows = latents.shape[0]
    group_count = lax.axis_size("dp")
    seq_count = lax.axis_size("seq")
    capacity = (max(2, 3 * local_rows // (2 * group_count)) + 15) // 16 * 16
    per_block = local_rows // TILE
    side = seq_count // 2
    half = group_count // 2
    me_dp = lax.axis_index("dp").astype(jnp.int32)[None]
    me_seq = lax.axis_index("seq").astype(jnp.int32)[None]
    single = [1 << i for i in reversed(range(half.bit_length() - 1))]
    several = [r for r in range(1, half) if r not in single]

    packed = pack(me_dp, target, latents, group_count, seq_count, capacity)
    incoming = [packed[0]]
    for r in range(1, group_count):
        incoming.append(swap(packed[r], "dp", r))
    order = [r for pair in zip(reversed(range(half, group_count)), reversed(range(half))) for r in pair]
    begun = [incoming[half - 1]]
    own = join([after(w_query, *begun), w_key, w_value])
    pieces = {0: own}

    def piece(r, *ahead):
        bit = r & -r
        return swap(after(pieces[r ^ bit], *ahead), "dp", bit)

    for r in single:
        pieces[r] = piece(r)
    segments = [segment_ids]
    for r in range(1, seq_count):
        segments.append(swap(after(segment_ids, incoming[half + 1]), "seq", r))
    meta, other, clip = marks(me_seq, segments, per_block)
    done = [pieces[r] for r in single] + [meta] + [incoming[r] for r in order]

    pieces[half] = swap(after(own, *done), "dp", half)
    for r in several:
        pieces[r] = piece(r, *done)
    ready = after(segment_ids, *done)
    quarter = local_rows // 4
    blocks = {}
    for pair in range(2):
        whole, *quarters = place_and_norm(
            clip_bucket, ready, [incoming[r] for r in order], mod_table, 2 * pair * quarter, quarter
        )
        blocks[0, "pair", pair] = whole
        for which, block in enumerate(quarters):
            blocks[0, "quarter", 2 * pair + which] = block

    def spread(relative, kind, part, distance, *ahead):
        moved = swap(after(blocks[relative, kind, part], *ahead), "seq", distance)
        blocks[relative ^ distance, kind, part] = moved
        return moved

    done = [
        pieces[half],
        spread(0, "quarter", 0, side),
        spread(0, "quarter", 1, side),
        blocks[0, "pair", 1],
        *[pieces[r] for r in several],
    ]
    for r in single:
        pieces[half ^ r] = piece(half ^ r, *done)
    for r in several:
        pieces[half ^ r] = piece(half ^ r, *[pieces[half ^ other] for other in single])
    me = jnp.concatenate([me_dp, me_seq])
    own_parts = [blocks[0, "pair", part] for part in range(2)]
    near_weights, begun = near_half(me, own_parts, [pieces[r] for r in range(half)])
    third = spread(0, "quarter", 2, side, *done)
    spread(0, "quarter", 3, side, *done)
    for part in range(2):
        spread(0, "pair", part, 1, third, near_weights)
    for part in range(4):
        spread(side, "quarter", part, 1, third, near_weights)

    def parts(r):
        kind, count = ("pair", 2) if r < side else ("quarter", 4)
        return [blocks[r, kind, part] for part in range(count)]

    first = project_first(
        me,
        near_weights,
        begun,
        own_parts,
        parts(side),
        [pieces[r] for r in range(half, group_count)],
        per_block,
    )
    *far, query, keys, values = project_and_attend(
        me,
        meta,
        other,
        clip,
        [part for r in range(1, seq_count, 2) for part in parts(r)],
        [near_weights, *first],
        group_count,
        seq_count,
        per_block,
    )
    near = attend_near(meta, other, query, keys, values, clip, side * per_block)
    outs = [near[r * per_block : (r + 1) * per_block] for r in range(side)]
    outs += [[block] for block in far]
    outs = [[swap(out, "seq", r) if r else out for out in group] for r, group in enumerate(outs)]
    return side_by_side(me_seq, outs)


def solution(mesh):
    in_specs = (
        P(("dp", "seq"), None),
        P(("dp", "seq")),
        P("dp", "seq"),
        P("dp", None),
        P(),
        P("dp", "seq"),
        P("dp", "seq"),
        P("dp", "seq"),
    )
    out_specs = P(("dp", "seq"), None)
    return jax.shard_map(
        on_device, mesh=mesh, in_specs=in_specs, out_specs=out_specs, check_vma=False
    )
```
